32 devices in a mesh: groups: 2 (over x), seq: 16 (over z, y, core).
Axes of the slice: x: 2, y: 2, z: 4, core: 2. Of those that a mesh axis runs over, the one named last changes fastest.
Arguments:
- queries: bfloat16 [10240, 4096], P(('groups', 'seq')), parts along dimension 0, may hold values from -6 to 6
- keys: bfloat16 [10240, 4096], P(('groups', 'seq')), parts along dimension 0, may hold values from -6 to 6
- values: bfloat16 [10240, 4096], P(('groups', 'seq')), parts along dimension 0, may hold values from -6 to 6
- doc_starts: int32 [32, 2], P(('groups', 'seq')), parts along dimension 0, may hold values from 0 to 320, as said below
- previous_window_states: bfloat16 [64, 32, 128, 128], P(('groups', 'seq')), parts along dimension 0, may hold values from -80 to 80
- out_gain: float32 [4096], replicated, may hold values from 0.1 to 1.9
Outputs:
- attended: bfloat16 [10240, 4096], P(('groups', 'seq')), parts along dimension 0
The draws below stay inside these ranges and needn't reach their ends.
There are 2 independent parts, one for each index of `groups`. The reference program is written for one: setup_inputs(seed, part) draws one part's arguments, and reference() takes and returns one part's arrays. A program takes and returns all parts, laid end to end along the dimension named above; an argument that names none is the same for every part. Nothing has to cross between parts.
Inputs may be any that keep to these rules, and one draw needn't show every extreme that they name: `doc_starts`: each row holds the offsets of document starts in that block of 320 tokens, ascending, with 320 in unused entries; row 0 begins with 0; every document has at most 3840 tokens, and one has exactly that many; some row holds 2 starts.
All inputs are finite; a program needn't handle non-finite values.
Results may differ from the reference program's by a relative error of at most 0.0049.
Values sent between devices are 32-bit elements; how exact they have to be, the bound alone decides.
A program may use at most 128 MiB of HBM per device.

```python
import jax
import jax.numpy as jnp
from jax import lax

HEAD_COUNT = 32
KEY_DIM = 128
VALUE_DIM = 128
BLOCK_TOKENS = 320
DOCUMENT_BLOCKS = 12
BMAX = 2
WINDOW_TOKENS = 5120
STATE_SLOTS = 32
N_SEQ = 16


def draw_doc_starts(key, part):
    key_count, key_first, key_second, key_plant, key_offset = jax.random.split(key, 5)
    blocks = jnp.arange(N_SEQ, dtype=jnp.int32)
    counts = jax.random.randint(key_count, (N_SEQ,), 0, 3)
    counts = jnp.where(blocks % 6 == 0, jnp.maximum(counts, 1), counts)
    counts = jnp.where(blocks == 0, 2, counts)
    first = jax.random.randint(key_first, (N_SEQ,), 0, BLOCK_TOKENS - 1)
    first = jnp.where(blocks == 0, 0, first)
    second = jax.random.randint(key_second, (N_SEQ,), first + 1, BLOCK_TOKENS)
    planted = jax.random.randint(key_plant, (), 1, N_SEQ - DOCUMENT_BLOCKS)
    offset = jax.random.randint(key_offset, (), 0, BLOCK_TOKENS)
    inside = (blocks > planted) & (blocks < planted + DOCUMENT_BLOCKS)
    ends = (blocks == planted) | (blocks == planted + DOCUMENT_BLOCKS)
    counts = jnp.where(inside, 0, jnp.where(ends, 1, counts))
    first = jnp.where(ends, offset, first)
    entry_one = jnp.where(counts >= 1, first, BLOCK_TOKENS)
    entry_two = jnp.where(counts == 2, second, BLOCK_TOKENS)
    return jnp.stack([entry_one, entry_two], axis=1).astype(jnp.int32)


def shard_levels(key, dims, pieces, low, top_value):
    def one(dim, blocks):
        draws = jax.random.uniform(jax.random.fold_in(jax.random.fold_in(key, 6), dim), (blocks,), jnp.float32, low / len(pieces), top_value / len(pieces))
        return jnp.repeat(jnp.exp(draws), dims[dim] // blocks).reshape((-1,) + (1,) * (len(dims) - dim - 1))

    level = one(*pieces[0])
    for cut in pieces[1:]:
        level = level * one(*cut)
    return level


def centred(stream_key, extent, deviation, limit, cuts=(), kind=jnp.bfloat16):
    entries = deviation * jax.random.normal(stream_key, extent, jnp.float32)
    if cuts:
        entries = entries * shard_levels(stream_key, extent, cuts, -0.22, 0.18)
    return jnp.clip(entries, -limit, limit).astype(kind)


def setup_inputs(seed: int = 0, part: int = 0) -> dict:
    key_of = jax.random.split(jax.random.key(seed), 7)
    part_splits = jax.random.split(jax.random.fold_in(key_of[6], part), 7)
    queries = centred(part_splits[0], (WINDOW_TOKENS, HEAD_COUNT * KEY_DIM), 1.0, 6.0, ((0, 16),))
    keys = centred(part_splits[1], (WINDOW_TOKENS, HEAD_COUNT * KEY_DIM), 1.0, 6.0, ((0, 16),))
    values = centred(part_splits[2], (WINDOW_TOKENS, HEAD_COUNT * VALUE_DIM), 1.0, 6.0, ((0, 16),))
    doc_starts = draw_doc_starts(jax.random.fold_in(jax.random.fold_in(key_of[6], part), 71), part)
    previous_window_states = centred(part_splits[4], (STATE_SLOTS, HEAD_COUNT, KEY_DIM, VALUE_DIM), ((BLOCK_TOKENS // 2) ** 0.5), 80.0, ((0, 16),))
    out_gain = jnp.clip(1.0 + 0.18 * jax.random.normal(key_of[5], (HEAD_COUNT * VALUE_DIM,), jnp.float32), 0.1, 1.9)
    return dict(queries=queries, keys=keys, values=values, doc_starts=doc_starts, previous_window_states=previous_window_states, out_gain=out_gain)


EPSILON = 1e-06

def features(raw):
    return jax.nn.silu(raw.astype(jnp.float32)).astype(jnp.bfloat16)

def segment_numbers(starts, rows_here):
    position = jnp.arange(rows_here, dtype=jnp.int32)
    segment = lax.optimization_barrier(jnp.sum((starts[None, :] <= position[:, None]).astype(jnp.int32), axis=1))
    last_segment = jnp.sum((starts < rows_here).astype(jnp.int32))
    return (position, segment, last_segment)

def block_terms(query_feat, key_feat, value_block, starts, carried_block):
    rows_here = query_feat.shape[0]
    position, segment, last_segment = segment_numbers(starts, rows_here)
    allowed = (position[:, None] >= position[None, :]) & (segment[:, None] == segment[None, :])
    query_wide = query_feat.astype(jnp.float32)
    key_wide = key_feat.astype(jnp.float32)
    value_wide = value_block.astype(jnp.float32)
    scores = jnp.einsum('thd,shd->hts', query_wide, key_wide, precision=lax.Precision.HIGHEST)
    scores = jnp.where(allowed[None], scores, 0.0).astype(jnp.bfloat16)
    within = jnp.einsum('hts,she->the', scores.astype(jnp.float32), value_wide, precision=lax.Precision.HIGHEST)
    initial = jnp.zeros(carried_block.shape[1:], jnp.float32)
    for member in range(carried_block.shape[0]):
        resumed = carried_block[member].astype(jnp.float32)
        term = jnp.einsum('thd,hde->the', query_wide, resumed, precision=lax.Precision.HIGHEST)
        within = within + jnp.where((segment == member + 1)[:, None, None], term, 0.0)
        initial = initial + jnp.where(last_segment == member + 1, resumed, 0.0)
    tail_keys = jnp.where((segment == last_segment)[:, None, None], key_wide, 0.0)
    summary = jnp.einsum('thd,the->hde', tail_keys, value_wide, precision=lax.Precision.HIGHEST) + initial
    started = jnp.reshape((last_segment > 0).astype(jnp.float32), (1,))
    return (query_wide, within, segment, started, summary)

def finish(query_wide, within, segment, incoming, out_gain):
    cross = jnp.einsum('thd,hde->the', query_wide, incoming, precision=lax.Precision.HIGHEST)
    total = within + jnp.where((segment == 0)[:, None, None], cross, 0.0)
    flat = total.reshape(total.shape[0], -1)
    mean_square = lax.optimization_barrier(jnp.mean(flat * flat, axis=1, keepdims=True))
    return (flat * lax.rsqrt(mean_square + EPSILON) * out_gain).astype(jnp.bfloat16)

def reference(queries, keys, values, doc_starts, previous_window_states, out_gain):
    query_all = features(queries).reshape(N_SEQ, BLOCK_TOKENS, HEAD_COUNT, KEY_DIM)
    key_all = features(keys).reshape(N_SEQ, BLOCK_TOKENS, HEAD_COUNT, KEY_DIM)
    value_all = values.reshape(N_SEQ, BLOCK_TOKENS, HEAD_COUNT, VALUE_DIM)
    carried_all = previous_window_states.reshape(N_SEQ, BMAX, HEAD_COUNT, KEY_DIM, VALUE_DIM)

    def advance(state_in, inputs):
        query_feat, key_feat, value_block, starts, carried_block = inputs
        query_wide, within, segment, started, summary = block_terms(query_feat, key_feat, value_block, starts, carried_block)
        output = finish(query_wide, within, segment, state_in, out_gain)
        state_out = jnp.where(started[0] > 0, summary, state_in + summary)
        return (state_out, output)
    initial_state = jnp.zeros((HEAD_COUNT, KEY_DIM, VALUE_DIM), jnp.float32)
    final_state, outputs = lax.scan(advance, initial_state, (query_all, key_all, value_all, doc_starts, carried_all))
    return outputs.reshape(WINDOW_TOKENS, HEAD_COUNT * VALUE_DIM)
```

```python
import functools

import jax
import jax.numpy as jnp
from jax import lax
from jax.experimental import pallas as pl
from jax.experimental.pallas import tpu as pltpu
from jax.sharding import PartitionSpec as P

HEADS = 32
DIM = 128
PART = HEADS // 4
EPSILON = 1e-06
LAG = 9
ROWS_OUT = 32
MESH = pl.DeviceIdType.MESH


def silu(x):
    half = x.astype(jnp.float32) * 0.5
    return (half + half * jnp.tanh(half)).astype(jnp.bfloat16)


def kernel(
    starts, q_hbm, k_hbm, v_hbm, c_hbm, gain, out_hbm,
    q, k, v, c, o, obuf, acc, allowed, seg_masks, flags, coefs,
    state, near_a, near_b, chip_out, chip_own, chip_in, row, z_in, z_out, back_out, back_in,
    final_a, final_b, incoming,
    in_sem, out_sem, flag_send, flag_recv, send_sem, recv_sem,
):
    rows = q.shape[0]
    count = lax.axis_size("seq")
    me = lax.axis_index("seq")
    z = me // 4
    depth = count // 4
    y = (me // 2) % 2
    core = me % 2
    partner = me + 1 - 2 * core
    across = me + 2 - 4 * y
    following = lax.rem(me + 4, count)
    mine = y * 2 + core
    part_near = y * 2 + (1 - core)
    part_far = (1 - y) * 2 + core
    part_diag = (1 - y) * 2 + (1 - core)

    def load(slot, source, target, part):
        columns = pl.ds(pl.multiple_of(part * (PART * DIM), PART * DIM), PART * DIM)
        return pltpu.make_async_copy(source.at[:, columns], target.at[:, columns], in_sem.at[slot])

    def load_states(slot, part):
        heads = pl.ds(part * PART, PART)
        return pltpu.make_async_copy(c_hbm.at[:, heads], c.at[:, heads], in_sem.at[slot])

    order_kv = (part_diag, part_far, part_near, mine)
    order_q = (mine, part_near, part_far, part_diag)
    k_loads = [load(i, k_hbm, k, p) for i, p in enumerate(order_kv)]
    v_loads = [load(4 + i, v_hbm, v, p) for i, p in enumerate(order_kv)]
    c_loads = [load_states(8 + i, p) for i, p in enumerate(order_kv)]
    q_loads = [load(12 + i, q_hbm, q, p) for i, p in enumerate(order_q)]
    for i in range(4):
        k_loads[i].start()
        v_loads[i].start()
        c_loads[i].start()
    for i in range(4):
        q_loads[i].start()

    barrier = pltpu.get_barrier_semaphore()
    for other in (partner, across):
        pl.semaphore_signal(barrier, inc=1, device_id={"seq": other}, device_id_type=MESH)

    @pl.when(z > 0)
    def _():
        pl.semaphore_signal(barrier, inc=1, device_id={"seq": me - 4}, device_id_type=MESH)

    @pl.when(z < depth - 1)
    def _():
        pl.semaphore_signal(barrier, inc=1, device_id={"seq": me + 4}, device_id_type=MESH)

    first, second = starts[0, 0], starts[0, 1]
    last = (first < rows).astype(jnp.int32) + (second < rows).astype(jnp.int32)
    take_one = jnp.where(last == 1, 1.0, 0.0)
    take_two = jnp.where(last == 2, 1.0, 0.0)
    here = jnp.where(last > 0, 1.0, 0.0)

    def segments(shape, dim):
        position = lax.broadcasted_iota(jnp.int32, shape, dim)
        one = jnp.where(position >= first, 1, 0)
        return position, one + jnp.where(position >= second, 1, 0)

    row_pos, row_seg = segments((rows, rows), 0)
    col_pos, col_seg = segments((rows, rows), 1)
    allowed[...] = jnp.where((row_pos >= col_pos) & (row_seg == col_seg), 1.0, 0.0)
    _, seg = segments((rows, DIM), 0)
    for i in range(3):
        seg_masks[i] = jnp.where(seg == i, 1.0, 0.0).astype(jnp.bfloat16)
    seg_masks[3] = jnp.where(seg == last, 1.0, 0.0).astype(jnp.bfloat16)
    acc[...] = jnp.zeros_like(acc)
    flags[0] = jnp.full((8, DIM), here, jnp.float32)

    @pl.when(z == 0)
    def _():
        z_in[...] = jnp.zeros_like(z_in)

    neighbours = 2 + jnp.where(z > 0, 1, 0) + jnp.where(z < depth - 1, 1, 0)
    pl.semaphore_wait(barrier, neighbours)

    def remote(kind, slot, source, target, device):
        return pltpu.make_async_remote_copy(
            src_ref=source, dst_ref=target, send_sem=send_sem.at[kind, slot],
            recv_sem=recv_sem.at[kind, slot], device_id={"seq": device}, device_id_type=MESH,
        )

    def flag_copy(slot, source, target, device):
        return pltpu.make_async_remote_copy(
            src_ref=flags.at[source], dst_ref=flags.at[target], send_sem=flag_send.at[slot],
            recv_sem=flag_recv.at[slot], device_id={"seq": device}, device_id_type=MESH,
        )

    def near_a_copy(i):
        return remote(0, i, state.at[part_diag * PART + i], near_a.at[i], partner)

    def near_b_copy(i):
        return remote(1, i, state.at[part_near * PART + i], near_b.at[i], partner)

    def chip_copy(i):
        return remote(2, i, chip_out.at[i], chip_in.at[i], across)

    def z_copy(i):
        return remote(3, i, z_out.at[i], z_in.at[i], following)

    def back_copy(i):
        return remote(4, i, back_out.at[i], back_in.at[i], across)

    def final_a_send(i):
        return remote(5, i, final_a.at[i], incoming.at[mine * PART + i], partner)

    def final_a_recv(i):
        return remote(5, i, final_a.at[i], incoming.at[part_near * PART + i], partner)

    def final_b_send(i):
        return remote(6, i, final_b.at[i], incoming.at[part_far * PART + i], partner)

    def final_b_recv(i):
        return remote(6, i, final_b.at[i], incoming.at[part_diag * PART + i], partner)

    near_flag = flag_copy(0, 0, 1, partner)
    near_flag.start()

    def lanes(head):
        return pl.ds(pl.multiple_of(head * DIM, DIM), DIM)

    def summarise(head):
        at = lanes(head)
        feature = silu(k[:, at])
        k[:, at] = feature
        total = lax.dot_general(
            feature * seg_masks[3], v[:, at], (((0,), (0,)), ((), ())),
            preferred_element_type=jnp.float32,
        )
        state[head] = (
            total + take_one * c[0, head].astype(jnp.float32)
            + take_two * c[1, head].astype(jnp.float32)
        )

    for i in range(2):
        k_loads[i].wait()
        v_loads[i].wait()
        c_loads[i].wait()

    summarise(part_diag * PART)
    near_a_copy(0).start()

    near_flag.wait_recv()
    is_one = jnp.where(core == 1, 1.0, 0.0)
    keep_me = 1.0 - flags[0]
    keep_near = 1.0 - flags[1]
    coefs[0] = jnp.where(core == 1, keep_me, keep_near)
    coefs[1] = jnp.where(core == 1, keep_near, keep_me)
    coefs[2] = keep_me * keep_near
    flags[2] = keep_me * keep_near
    across_flag = flag_copy(1, 2, 3, across)
    across_flag.start()

    def chip_sum(head, near):
        keep = coefs[0, 0:1, :]
        own_scale = jnp.where(core == 1, jnp.ones_like(keep), keep)
        near_scale = jnp.where(core == 1, keep, jnp.ones_like(keep))
        return state[head] * own_scale + near * near_scale

    @pl.loop(0, PART)
    def _(i):
        @pl.when(i < PART - 1)
        def _():
            summarise(part_diag * PART + i + 1)
            near_a_copy(i + 1).start()

        summarise(part_far * PART + i)
        near_a_copy(i).wait_recv()
        chip_out[i] = chip_sum(part_far * PART + i, near_a[i])
        chip_copy(i).start()

    for i in range(2, 4):
        k_loads[i].wait()
        v_loads[i].wait()
        c_loads[i].wait()
    summarise(part_near * PART)
    near_b_copy(0).start()
    across_flag.wait_recv()
    own_keep = coefs[2]
    far_keep = flags[3]
    coefs[3] = jnp.where(y == 0, own_keep, far_keep)
    coefs[4] = jnp.where(y == 0, far_keep, own_keep)
    coefs[5] = own_keep * far_keep

    @pl.loop(0, PART)
    def _(i):
        @pl.when(i < PART - 1)
        def _():
            summarise(part_near * PART + i + 1)
            near_b_copy(i + 1).start()

        summarise(mine * PART + i)
        near_b_copy(i).wait_recv()
        chip_own[i] = chip_sum(mine * PART + i, near_b[i])

    def local(head):
        at = lanes(head)
        feature = silu(q[:, at])
        q[:, at] = feature * seg_masks[0]
        scores = lax.dot_general(
            feature, k[:, at], (((1,), (1,)), ((), ())), preferred_element_type=jnp.float32
        )
        scores = (scores * allowed[...]).astype(jnp.bfloat16)
        resumed = jnp.concatenate([feature * seg_masks[1], feature * seg_masks[2]], axis=1)
        carried = jnp.concatenate([c[0, head], c[1, head]], axis=0)
        o[:, at] = jnp.dot(scores, v[:, at], preferred_element_type=jnp.float32) + jnp.dot(
            resumed, carried, preferred_element_type=jnp.float32
        )

    def cross(head):
        at = lanes(head)
        wide = incoming[head]
        high = wide.astype(jnp.bfloat16)
        low = (wide - high.astype(jnp.float32)).astype(jnp.bfloat16)
        query = q[:, at]
        total = o[:, at] + jnp.dot(
            jnp.concatenate([query, query], axis=1),
            jnp.concatenate([high, low], axis=0),
            preferred_element_type=jnp.float32,
        )
        o[:, at] = total
        acc[...] += total * total

    def pair(chip_state, head, near):
        keep = coefs[1, 0:1, :]
        one = jnp.ones_like(keep)
        zero = jnp.zeros_like(keep)
        at_one = core == 1
        own = chip_state * jnp.where(at_one, keep, one) + near * jnp.where(at_one, one, zero)
        other = chip_state * jnp.where(at_one, one, keep) + state[head] * jnp.where(
            at_one, zero, one
        )
        return own, other

    def row_step(i):
        chip_copy(i).wait_recv()
        keep = coefs[4, 0:1, :]
        one = jnp.ones_like(keep)
        row[i] = chip_own[i] * jnp.where(y == 0, keep, one) + chip_in[i] * jnp.where(
            y == 0, one, keep
        )

    def prefix_step(i):
        @pl.when(z > 0)
        def _():
            z_copy(i).wait_recv()

        before = z_in[i]
        z_out[i] = row[i] + before * coefs[5, 0:1, :]

        @pl.when(z < depth - 1)
        def _():
            z_copy(i).start()

        keep = coefs[3, 0:1, :]
        one = jnp.ones_like(keep)
        zero = jnp.zeros_like(keep)
        at_one = y == 1
        back_out[i] = before * jnp.where(at_one, one, keep) + chip_own[i] * jnp.where(
            at_one, zero, one
        )
        back_copy(i).start()
        chip_state = before * jnp.where(at_one, keep, one) + chip_in[i] * jnp.where(
            at_one, one, zero
        )
        head = mine * PART + i
        own, other = pair(chip_state, head, near_b[i])
        final_a[i] = other
        final_a_send(i).start()
        incoming[head] = own
        cross(head)

    def near_step(i):
        final_a_recv(i).wait_recv()
        cross(part_near * PART + i)

    def back_step(i):
        back_copy(i).wait_recv()
        head = part_far * PART + i
        own, other = pair(back_in[i], head, near_a[i])
        final_b[i] = other
        final_b_send(i).start()
        incoming[head] = own
        cross(head)

    def diag_step(i):
        final_b_recv(i).wait_recv()
        cross(part_diag * PART + i)

    skew = jnp.minimum(2 * z, 6)
    for i in range(4):
        q_loads[i].wait()

    @pl.loop(0, PART + LAG + 1)
    def _(t):
        @pl.when(t < PART)
        def _():
            local(mine * PART + t)
            local(part_near * PART + t)
            row_step(t)

        @pl.when((t >= PART) & (t < 2 * PART))
        def _():
            local(part_far * PART + t - PART)
            local(part_diag * PART + t - PART)

        @pl.when((t >= skew) & (t < skew + PART))
        def _():
            prefix_step(t - skew)

        @pl.when((t >= skew + 1) & (t < skew + 1 + PART))
        def _():
            near_step(t - skew - 1)

        @pl.when((t >= LAG) & (t < LAG + PART))
        def _():
            back_step(t - LAG)

        @pl.when(t >= LAG + 1)
        def _():
            diag_step(t - LAG - 1)

    def out_copy(i):
        span = pl.ds(pl.multiple_of(i * ROWS_OUT, ROWS_OUT), ROWS_OUT)
        return pltpu.make_async_copy(obuf.at[span], out_hbm.at[span], out_sem.at[i])

    @pl.loop(0, rows // ROWS_OUT)
    def _(i):
        span = pl.ds(pl.multiple_of(i * ROWS_OUT, ROWS_OUT), ROWS_OUT)
        square = jnp.sum(acc[span, :], axis=1, keepdims=True) * (1.0 / (HEADS * DIM))
        scale = lax.rsqrt(square + EPSILON)
        obuf[span, :] = (o[span, :] * scale * gain[...]).astype(jnp.bfloat16)
        out_copy(i).start()

    near_flag.wait_send()
    across_flag.wait_send()

    @pl.loop(0, PART)
    def _(i):
        near_a_copy(i).wait_send()
        near_b_copy(i).wait_send()
        chip_copy(i).wait_send()

        @pl.when(z < depth - 1)
        def _():
            z_copy(i).wait_send()

        back_copy(i).wait_send()
        final_a_send(i).wait_send()
        final_b_send(i).wait_send()

    @pl.loop(0, rows // ROWS_OUT)
    def _(i):
        out_copy(i).wait()


def on_device(queries, keys, values, doc_starts, previous_window_states, out_gain):
    rows, width = queries.shape
    bf16, f32 = jnp.bfloat16, jnp.float32
    part = pltpu.VMEM((PART, DIM, DIM), f32)
    everywhere = pl.BlockSpec(memory_space=pl.ANY)
    return pl.pallas_call(
        kernel,
        out_shape=jax.ShapeDtypeStruct((rows, width), bf16),
        in_specs=[pl.BlockSpec(memory_space=pltpu.SMEM)] + [everywhere] * 4
        + [pl.BlockSpec(memory_space=pltpu.VMEM)],
        out_specs=everywhere,
        scratch_shapes=[
            pltpu.VMEM((rows, width), bf16),
            pltpu.VMEM((rows, width), bf16),
            pltpu.VMEM((rows, width), bf16),
            pltpu.VMEM((2, HEADS, DIM, DIM), bf16),
            pltpu.VMEM((rows, width), f32),
            pltpu.VMEM((rows, width), bf16),
            pltpu.VMEM((rows, DIM), f32),
            pltpu.VMEM((rows, rows), f32),
            pltpu.VMEM((4, rows, DIM), bf16),
            pltpu.VMEM((4, 8, DIM), f32),
            pltpu.VMEM((6, 8, DIM), f32),
            pltpu.VMEM((HEADS, DIM, DIM), f32),
        ] + [part] * 12 + [
            pltpu.VMEM((HEADS, DIM, DIM), f32),
            pltpu.SemaphoreType.DMA((16,)),
            pltpu.SemaphoreType.DMA((rows // ROWS_OUT,)),
            pltpu.SemaphoreType.DMA((2,)),
            pltpu.SemaphoreType.DMA((2,)),
            pltpu.SemaphoreType.DMA((7, PART)),
            pltpu.SemaphoreType.DMA((7, PART)),
        ],
        compiler_params=pltpu.CompilerParams(
            collective_id=0, has_side_effects=True, vmem_limit_bytes=56 * 1024 * 1024
        ),
        cost_estimate=pl.CostEstimate(
            flops=4 * 10**9, bytes_accessed=13 * 10**6, transcendentals=3 * 10**6
        ),
    )(doc_starts, queries, keys, values, previous_window_states, out_gain.reshape(1, width))


def solution(mesh):
    placed = (
        P(("groups", "seq"), None),
        P(("groups", "seq"), None),
        P(("groups", "seq"), None),
        P(("groups", "seq"), None),
        P(("groups", "seq"), None, None, None),
        P(),
    )
    return jax.shard_map(
        on_device, mesh=mesh, in_specs=placed, out_specs=P(("groups", "seq"), None), check_vma=False
    )
```

```python
import jax
import jax.numpy as jnp
from jax import lax
from jax.experimental import pallas as pl
from jax.experimental.pallas import tpu as pltpu
from jax.sharding import PartitionSpec as P

HEADS = 32
DIM = 128
PART = HEADS // 4
EPSILON = 1e-06
LAG = 9
MESH = pl.DeviceIdType.MESH


def silu(x):
    half = x.astype(jnp.float32) * 0.5
    return (half + half * jnp.tanh(half)).astype(jnp.bfloat16)


def kernel(
    starts, q_hbm, k_hbm, v_hbm, c_hbm, out_hbm, acc,
    q, k, v, c, o, obuf, allowed, seg_masks, flags, coefs,
    state, near_a, near_b, chip_out, chip_own, chip_in, row, z_in, z_out, back_out, back_in,
    final_a, final_b, incoming,
    in_sem, out_sem, flag_send, flag_recv, send_sem, recv_sem,
):
    rows = q.shape[0]
    count = lax.axis_size("seq")
    me = lax.axis_index("seq")
    z = me // 4
    depth = count // 4
    y = (me // 2) % 2
    core = me % 2
    partner = me + 1 - 2 * core
    across = me + 2 - 4 * y
    following = lax.rem(me + 4, count)
    mine = y * 2 + core
    part_near = y * 2 + (1 - core)
    part_far = (1 - y) * 2 + core
    part_diag = (1 - y) * 2 + (1 - core)

    def load(slot, source, target, part):
        columns = pl.ds(pl.multiple_of(part * (PART * DIM), PART * DIM), PART * DIM)
        return pltpu.make_async_copy(source.at[:, columns], target.at[:, columns], in_sem.at[slot])

    def load_states(slot, part):
        heads = pl.ds(part * PART, PART)
        return pltpu.make_async_copy(c_hbm.at[:, heads], c.at[:, heads], in_sem.at[slot])

    order_kv = (part_diag, part_far, part_near, mine)
    order_q = (mine, part_near, part_far, part_diag)
    k_loads = [load(i, k_hbm, k, p) for i, p in enumerate(order_kv)]
    v_loads = [load(4 + i, v_hbm, v, p) for i, p in enumerate(order_kv)]
    c_loads = [load_states(8 + i, p) for i, p in enumerate(order_kv)]
    q_loads = [load(12 + i, q_hbm, q, p) for i, p in enumerate(order_q)]
    for i in range(4):
        k_loads[i].start()
        v_loads[i].start()
        c_loads[i].start()
    for i in range(4):
        q_loads[i].start()

    barrier = pltpu.get_barrier_semaphore()
    for other in (partner, across):
        pl.semaphore_signal(barrier, inc=1, device_id={"seq": other}, device_id_type=MESH)

    @pl.when(z > 0)
    def _():
        pl.semaphore_signal(barrier, inc=1, device_id={"seq": me - 4}, device_id_type=MESH)

    @pl.when(z < depth - 1)
    def _():
        pl.semaphore_signal(barrier, inc=1, device_id={"seq": me + 4}, device_id_type=MESH)

    first, second = starts[0, 0], starts[0, 1]
    last = (first < rows).astype(jnp.int32) + (second < rows).astype(jnp.int32)
    take_one = jnp.where(last == 1, 1.0, 0.0)
    take_two = jnp.where(last == 2, 1.0, 0.0)
    here = jnp.where(last > 0, 1.0, 0.0)

    def segments(shape, dim):
        position = lax.broadcasted_iota(jnp.int32, shape, dim)
        one = jnp.where(position >= first, 1, 0)
        return position, one + jnp.where(position >= second, 1, 0)

    row_pos, row_seg = segments((rows, rows), 0)
    col_pos, col_seg = segments((rows, rows), 1)
    allowed[...] = jnp.where((row_pos >= col_pos) & (row_seg == col_seg), 1.0, 0.0)
    _, seg = segments((rows, DIM), 0)
    for i in range(3):
        seg_masks[i] = jnp.where(seg == i, 1.0, 0.0).astype(jnp.bfloat16)
    seg_masks[3] = jnp.where(seg == last, 1.0, 0.0).astype(jnp.bfloat16)
    acc[...] = jnp.zeros_like(acc)
    flags[0] = jnp.full((8, DIM), here, jnp.float32)

    @pl.when(z == 0)
    def _():
        z_in[...] = jnp.zeros_like(z_in)

    neighbours = 2 + jnp.where(z > 0, 1, 0) + jnp.where(z < depth - 1, 1, 0)
    pl.semaphore_wait(barrier, neighbours)

    def remote(kind, slot, source, target, device):
        return pltpu.make_async_remote_copy(
            src_ref=source, dst_ref=target, send_sem=send_sem.at[kind, slot],
            recv_sem=recv_sem.at[kind, slot], device_id={"seq": device}, device_id_type=MESH,
        )

    def flag_copy(slot, source, target, device):
        return pltpu.make_async_remote_copy(
            src_ref=flags.at[source], dst_ref=flags.at[target], send_sem=flag_send.at[slot],
            recv_sem=flag_recv.at[slot], device_id={"seq": device}, device_id_type=MESH,
        )

    def near_a_copy(i):
        return remote(0, i, state.at[part_diag * PART + i], near_a.at[i], partner)

    def near_b_copy(i):
        return remote(1, i, state.at[part_near * PART + i], near_b.at[i], partner)

    def chip_copy(i):
        return remote(2, i, chip_out.at[i], chip_in.at[i], across)

    def z_copy(i):
        return remote(3, i, z_out.at[i], z_in.at[i], following)

    def back_copy(i):
        return remote(4, i, back_out.at[i], back_in.at[i], across)

    def final_a_send(i):
        return remote(5, i, final_a.at[i], incoming.at[mine * PART + i], partner)

    def final_a_recv(i):
        return remote(5, i, final_a.at[i], incoming.at[part_near * PART + i], partner)

    def final_b_send(i):
        return remote(6, i, final_b.at[i], incoming.at[part_far * PART + i], partner)

    def final_b_recv(i):
        return remote(6, i, final_b.at[i], incoming.at[part_diag * PART + i], partner)

    near_flag = flag_copy(0, 0, 1, partner)
    near_flag.start()

    def lanes(head):
        return pl.ds(pl.multiple_of(head * DIM, DIM), DIM)

    def summarise(head):
        at = lanes(head)
        feature = silu(k[:, at])
        k[:, at] = feature
        total = lax.dot_general(
            feature * seg_masks[3], v[:, at], (((0,), (0,)), ((), ())),
            preferred_element_type=jnp.float32,
        )
        state[head] = (
            total + take_one * c[0, head].astype(jnp.float32)
            + take_two * c[1, head].astype(jnp.float32)
        )

    for i in range(2):
        k_loads[i].wait()
        v_loads[i].wait()
        c_loads[i].wait()

    summarise(part_diag * PART)
    near_a_copy(0).start()

    near_flag.wait_recv()
    is_one = jnp.where(core == 1, 1.0, 0.0)
    keep_me = 1.0 - flags[0]
    keep_near = 1.0 - flags[1]
    coefs[0] = jnp.where(core == 1, keep_me, keep_near)
    coefs[1] = jnp.where(core == 1, keep_near, keep_me)
    coefs[2] = keep_me * keep_near
    flags[2] = keep_me * keep_near
    across_flag = flag_copy(1, 2, 3, across)
    across_flag.start()

    def chip_sum(head, near):
        keep = coefs[0, 0:1, :]
        own_scale = jnp.where(core == 1, jnp.ones_like(keep), keep)
        near_scale = jnp.where(core == 1, keep, jnp.ones_like(keep))
        return state[head] * own_scale + near * near_scale

    @pl.loop(0, PART)
    def _(i):
        @pl.when(i < PART - 1)
        def _():
            summarise(part_diag * PART + i + 1)
            near_a_copy(i + 1).start()

        summarise(part_far * PART + i)
        near_a_copy(i).wait_recv()
        chip_out[i] = chip_sum(part_far * PART + i, near_a[i])
        chip_copy(i).start()

    for i in range(2, 4):
        k_loads[i].wait()
        v_loads[i].wait()
        c_loads[i].wait()
    summarise(part_near * PART)
    near_b_copy(0).start()
    across_flag.wait_recv()
    own_keep = coefs[2]
    far_keep = flags[3]
    coefs[3] = jnp.where(y == 0, own_keep, far_keep)
    coefs[4] = jnp.where(y == 0, far_keep, own_keep)
    coefs[5] = own_keep * far_keep

    @pl.loop(0, PART)
    def _(i):
        @pl.when(i < PART - 1)
        def _():
            summarise(part_near * PART + i + 1)
            near_b_copy(i + 1).start()

        summarise(mine * PART + i)
        near_b_copy(i).wait_recv()
        chip_own[i] = chip_sum(mine * PART + i, near_b[i])

    def local(head):
        at = lanes(head)
        feature = silu(q[:, at])
        q[:, at] = feature * seg_masks[0]
        scores = lax.dot_general(
            feature, k[:, at], (((1,), (1,)), ((), ())), preferred_element_type=jnp.float32
        )
        scores = (scores * allowed[...]).astype(jnp.bfloat16)
        resumed = jnp.concatenate([feature * seg_masks[1], feature * seg_masks[2]], axis=1)
        carried = jnp.concatenate([c[0, head], c[1, head]], axis=0)
        o[:, at] = jnp.dot(scores, v[:, at], preferred_element_type=jnp.float32) + jnp.dot(
            resumed, carried, preferred_element_type=jnp.float32
        )

    def out_copy(head):
        at = lanes(head)
        return pltpu.make_async_copy(obuf.at[:, at], out_hbm.at[:, at], out_sem.at[head])

    def cross(head):
        at = lanes(head)
        wide = incoming[head]
        high = wide.astype(jnp.bfloat16)
        low = (wide - high.astype(jnp.float32)).astype(jnp.bfloat16)
        query = q[:, at]
        total = o[:, at] + jnp.dot(
            jnp.concatenate([query, query], axis=1),
            jnp.concatenate([high, low], axis=0),
            preferred_element_type=jnp.float32,
        )
        acc[...] += total * total
        obuf[:, at] = total.astype(jnp.bfloat16)
        out_copy(head).start()

    def pair(chip_state, head, near):
        keep = coefs[1, 0:1, :]
        one = jnp.ones_like(keep)
        zero = jnp.zeros_like(keep)
        at_one = core == 1
        own = chip_state * jnp.where(at_one, keep, one) + near * jnp.where(at_one, one, zero)
        other = chip_state * jnp.where(at_one, one, keep) + state[head] * jnp.where(
            at_one, zero, one
        )
        return own, other

    def row_step(i):
        chip_copy(i).wait_recv()
        keep = coefs[4, 0:1, :]
        one = jnp.ones_like(keep)
        row[i] = chip_own[i] * jnp.where(y == 0, keep, one) + chip_in[i] * jnp.where(
            y == 0, one, keep
        )

    def prefix_step(i):
        @pl.when(z > 0)
        def _():
            z_copy(i).wait_recv()

        before = z_in[i]
        z_out[i] = row[i] + before * coefs[5, 0:1, :]

        @pl.when(z < depth - 1)
        def _():
            z_copy(i).start()

        keep = coefs[3, 0:1, :]
        one = jnp.ones_like(keep)
        zero = jnp.zeros_like(keep)
        at_one = y == 1
        back_out[i] = before * jnp.where(at_one, one, keep) + chip_own[i] * jnp.where(
            at_one, zero, one
        )
        back_copy(i).start()
        chip_state = before * jnp.where(at_one, keep, one) + chip_in[i] * jnp.where(
            at_one, one, zero
        )
        head = mine * PART + i
        own, other = pair(chip_state, head, near_b[i])
        final_a[i] = other
        final_a_send(i).start()
        incoming[head] = own
        cross(head)

    def near_step(i):
        final_a_recv(i).wait_recv()
        cross(part_near * PART + i)

    def back_step(i):
        back_copy(i).wait_recv()
        head = part_far * PART + i
        own, other = pair(back_in[i], head, near_a[i])
        final_b[i] = other
        final_b_send(i).start()
        incoming[head] = own
        cross(head)

    def diag_step(i):
        final_b_recv(i).wait_recv()
        cross(part_diag * PART + i)

    skew = jnp.minimum(2 * z, 6)
    for i in range(4):
        q_loads[i].wait()

    @pl.loop(0, PART + LAG + 1)
    def _(t):
        @pl.when(t < PART)
        def _():
            local(mine * PART + t)
            local(part_near * PART + t)
            row_step(t)

        @pl.when((t >= PART) & (t < 2 * PART))
        def _():
            local(part_far * PART + t - PART)
            local(part_diag * PART + t - PART)

        @pl.when((t >= skew) & (t < skew + PART))
        def _():
            prefix_step(t - skew)

        @pl.when((t >= skew + 1) & (t < skew + 1 + PART))
        def _():
            near_step(t - skew - 1)

        @pl.when((t >= LAG) & (t < LAG + PART))
        def _():
            back_step(t - LAG)

        @pl.when(t >= LAG + 1)
        def _():
            diag_step(t - LAG - 1)

    near_flag.wait_send()
    across_flag.wait_send()

    @pl.loop(0, PART)
    def _(i):
        near_a_copy(i).wait_send()
        near_b_copy(i).wait_send()
        chip_copy(i).wait_send()

        @pl.when(z < depth - 1)
        def _():
            z_copy(i).wait_send()

        back_copy(i).wait_send()
        final_a_send(i).wait_send()
        final_b_send(i).wait_send()

    @pl.loop(0, HEADS)
    def _(i):
        out_copy(i).wait()


def on_device(queries, keys, values, doc_starts, previous_window_states, out_gain):
    rows, width = queries.shape
    bf16, f32 = jnp.bfloat16, jnp.float32
    part = pltpu.VMEM((PART, DIM, DIM), f32)
    everywhere = pl.BlockSpec(memory_space=pl.ANY)
    total, square = pl.pallas_call(
        kernel,
        out_shape=(
            jax.ShapeDtypeStruct((rows, width), bf16),
            jax.ShapeDtypeStruct((rows, DIM), f32),
        ),
        in_specs=[pl.BlockSpec(memory_space=pltpu.SMEM)] + [everywhere] * 4,
        out_specs=(everywhere, pl.BlockSpec(memory_space=pltpu.VMEM)),
        scratch_shapes=[
            pltpu.VMEM((rows, width), bf16),
            pltpu.VMEM((rows, width), bf16),
            pltpu.VMEM((rows, width), bf16),
            pltpu.VMEM((2, HEADS, DIM, DIM), bf16),
            pltpu.VMEM((rows, width), f32),
            pltpu.VMEM((rows, width), bf16),
            pltpu.VMEM((rows, rows), f32),
            pltpu.VMEM((4, rows, DIM), bf16),
            pltpu.VMEM((4, 8, DIM), f32),
            pltpu.VMEM((6, 8, DIM), f32),
            pltpu.VMEM((HEADS, DIM, DIM), f32),
        ] + [part] * 12 + [
            pltpu.VMEM((HEADS, DIM, DIM), f32),
            pltpu.SemaphoreType.DMA((16,)),
            pltpu.SemaphoreType.DMA((HEADS,)),
            pltpu.SemaphoreType.DMA((2,)),
            pltpu.SemaphoreType.DMA((2,)),
            pltpu.SemaphoreType.DMA((7, PART)),
            pltpu.SemaphoreType.DMA((7, PART)),
        ],
        compiler_params=pltpu.CompilerParams(
            collective_id=0, has_side_effects=True, vmem_limit_bytes=56 * 1024 * 1024
        ),
        cost_estimate=pl.CostEstimate(
            flops=4 * 10**9, bytes_accessed=13 * 10**6, transcendentals=3 * 10**6
        ),
    )(doc_starts, queries, keys, values, previous_window_states)
    mean_square = jnp.sum(square, axis=1, keepdims=True) / width
    return (total.astype(f32) * lax.rsqrt(mean_square + EPSILON) * out_gain).astype(bf16)


def solution(mesh):
    placed = (
        P(("groups", "seq"), None),
        P(("groups", "seq"), None),
        P(("groups", "seq"), None),
        P(("groups", "seq"), None),
        P(("groups", "seq"), None, None, None),
        P(),
    )
    return jax.shard_map(
        on_device, mesh=mesh, in_specs=placed, out_specs=P(("groups", "seq"), None), check_vma=False
    )
```

```python
import jax
import jax.numpy as jnp
from jax import lax
from jax.experimental import pallas as pl
from jax.experimental.pallas import tpu as pltpu
from jax.sharding import PartitionSpec as P

HEADS = 32
DIM = 128
PART = HEADS // 4
EPSILON = 1e-06
LAG = 9
ROWS_OUT = 32
MESH = pl.DeviceIdType.MESH


def silu(x):
    half = x.astype(jnp.float32) * 0.5
    return (half + half * jnp.tanh(half)).astype(jnp.bfloat16)


def kernel(
    starts, q_hbm, k_hbm, v_hbm, c_hbm, gain, out_hbm,
    q, k, v, c, o, obuf, acc, allowed, seg_masks, flags, coefs,
    state, near_a, near_b, chip_out, chip_own, chip_in, row, z_in, z_out, back_out, back_in,
    final_a, final_b, incoming,
    in_sem, out_sem, flag_send, flag_recv, send_sem, recv_sem,
):
    rows = q.shape[0]
    count = lax.axis_size("seq")
    me = lax.axis_index("seq")
    z = me // 4
    depth = count // 4
    y = (me // 2) % 2
    core = me % 2
    partner = me + 1 - 2 * core
    across = me + 2 - 4 * y
    following = lax.rem(me + 4, count)
    mine = y * 2 + core
    part_near = y * 2 + (1 - core)
    part_far = (1 - y) * 2 + core
    part_diag = (1 - y) * 2 + (1 - core)

    def load(slot, source, target, part):
        columns = pl.ds(pl.multiple_of(part * (PART * DIM), PART * DIM), PART * DIM)
        return pltpu.make_async_copy(source.at[:, columns], target.at[:, columns], in_sem.at[slot])

    def load_states(slot, part):
        heads = pl.ds(part * PART, PART)
        return pltpu.make_async_copy(c_hbm.at[:, heads], c.at[:, heads], in_sem.at[slot])

    order_kv = (part_diag, part_far, part_near, mine)
    order_q = (mine, part_near, part_far, part_diag)
    k_loads = [load(i, k_hbm, k, p) for i, p in enumerate(order_kv)]
    v_loads = [load(4 + i, v_hbm, v, p) for i, p in enumerate(order_kv)]
    c_loads = [load_states(8 + i, p) for i, p in enumerate(order_kv)]
    q_loads = [load(12 + i, q_hbm, q, p) for i, p in enumerate(order_q)]
    for i in range(4):
        k_loads[i].start()
        v_loads[i].start()
        c_loads[i].start()
    for i in range(4):
        q_loads[i].start()

    barrier = pltpu.get_barrier_semaphore()
    for other in (partner, across):
        pl.semaphore_signal(barrier, inc=1, device_id={"seq": other}, device_id_type=MESH)

    @pl.when(z > 0)
    def _():
        pl.semaphore_signal(barrier, inc=1, device_id={"seq": me - 4}, device_id_type=MESH)

    @pl.when(z < depth - 1)
    def _():
        pl.semaphore_signal(barrier, inc=1, device_id={"seq": me + 4}, device_id_type=MESH)

    first, second = starts[0, 0], starts[0, 1]
    last = (first < rows).astype(jnp.int32) + (second < rows).astype(jnp.int32)
    take_one = jnp.where(last == 1, 1.0, 0.0)
    take_two = jnp.where(last == 2, 1.0, 0.0)
    here = jnp.where(last > 0, 1.0, 0.0)

    def segments(shape, dim):
        position = lax.broadcasted_iota(jnp.int32, shape, dim)
        one = jnp.where(position >= first, 1, 0)
        return position, one + jnp.where(position >= second, 1, 0)

    row_pos, row_seg = segments((rows, rows), 0)
    col_pos, col_seg = segments((rows, rows), 1)
    allowed[...] = jnp.where((row_pos >= col_pos) & (row_seg == col_seg), 1.0, 0.0)
    _, seg = segments((rows, DIM), 0)
    for i in range(3):
        seg_masks[i] = jnp.where(seg == i, 1.0, 0.0).astype(jnp.bfloat16)
    seg_masks[3] = jnp.where(seg == last, 1.0, 0.0).astype(jnp.bfloat16)
    acc[...] = jnp.zeros_like(acc)
    flags[0] = jnp.full((8, DIM), here, jnp.float32)

    @pl.when(z == 0)
    def _():
        z_in[...] = jnp.zeros_like(z_in)

    neighbours = 2 + jnp.where(z > 0, 1, 0) + jnp.where(z < depth - 1, 1, 0)
    pl.semaphore_wait(barrier, neighbours)

    def remote(kind, slot, source, target, device):
        return pltpu.make_async_remote_copy(
            src_ref=source, dst_ref=target, send_sem=send_sem.at[kind, slot],
            recv_sem=recv_sem.at[kind, slot], device_id={"seq": device}, device_id_type=MESH,
        )

    def flag_copy(slot, source, target, device):
        return pltpu.make_async_remote_copy(
            src_ref=flags.at[source], dst_ref=flags.at[target], send_sem=flag_send.at[slot],
            recv_sem=flag_recv.at[slot], device_id={"seq": device}, device_id_type=MESH,
        )

    def near_a_copy(i):
        return remote(0, i, state.at[part_diag * PART + i], near_a.at[i], partner)

    def near_b_copy(i):
        return remote(1, i, state.at[part_near * PART + i], near_b.at[i], partner)

    def chip_copy(i):
        return remote(2, i, chip_out.at[i], chip_in.at[i], across)

    def z_copy(i):
        return remote(3, i, z_out.at[i], z_in.at[i], following)

    def back_copy(i):
        return remote(4, i, back_out.at[i], back_in.at[i], across)

    def final_a_send(i):
        return remote(5, i, final_a.at[i], incoming.at[mine * PART + i], partner)

    def final_a_recv(i):
        return remote(5, i, final_a.at[i], incoming.at[part_near * PART + i], partner)

    def final_b_send(i):
        return remote(6, i, final_b.at[i], incoming.at[part_far * PART + i], partner)

    def final_b_recv(i):
        return remote(6, i, final_b.at[i], incoming.at[part_diag * PART + i], partner)

    near_flag = flag_copy(0, 0, 1, partner)
    near_flag.start()

    def lanes(head):
        return pl.ds(pl.multiple_of(head * DIM, DIM), DIM)

    def summarise(*heads):
        features = [silu(k[:, lanes(head)]) for head in heads]
        tails = [feature * seg_masks[3] for feature in features]
        totals = [
            lax.dot_general(
                tail, v[:, lanes(head)], (((0,), (0,)), ((), ())),
                preferred_element_type=jnp.float32,
            )
            + take_one * c[0, head].astype(jnp.float32)
            + take_two * c[1, head].astype(jnp.float32)
            for tail, head in zip(tails, heads)
        ]
        for head, feature, total in zip(heads, features, totals):
            k[:, lanes(head)] = feature
            state[head] = total

    def arrive(i):
        k_loads[i].wait()
        v_loads[i].wait()
        c_loads[i].wait()

    arrive(0)
    summarise(part_diag * PART)
    near_a_copy(0).start()
    arrive(1)

    near_flag.wait_recv()
    is_one = jnp.where(core == 1, 1.0, 0.0)
    keep_me = 1.0 - flags[0]
    keep_near = 1.0 - flags[1]
    coefs[0] = jnp.where(core == 1, keep_me, keep_near)
    coefs[1] = jnp.where(core == 1, keep_near, keep_me)
    coefs[2] = keep_me * keep_near
    flags[2] = keep_me * keep_near
    across_flag = flag_copy(1, 2, 3, across)
    across_flag.start()

    def chip_sum(head, near):
        keep = coefs[0, 0:1, :]
        own_scale = jnp.where(core == 1, jnp.ones_like(keep), keep)
        near_scale = jnp.where(core == 1, keep, jnp.ones_like(keep))
        return state[head] * own_scale + near * near_scale

    def chip_step(i):
        near_a_copy(i).wait_recv()
        chip_out[i] = chip_sum(part_far * PART + i, near_a[i])
        chip_copy(i).start()

    @pl.loop(0, PART - 1)
    def _(i):
        summarise(part_diag * PART + i + 1, part_far * PART + i)
        near_a_copy(i + 1).start()
        chip_step(i)

    summarise(part_far * PART + PART - 1)
    chip_step(PART - 1)

    arrive(2)
    arrive(3)
    summarise(part_near * PART)
    near_b_copy(0).start()
    across_flag.wait_recv()
    own_keep = coefs[2]
    far_keep = flags[3]
    coefs[3] = jnp.where(y == 0, own_keep, far_keep)
    coefs[4] = jnp.where(y == 0, far_keep, own_keep)
    coefs[5] = own_keep * far_keep

    def own_step(i):
        near_b_copy(i).wait_recv()
        chip_own[i] = chip_sum(mine * PART + i, near_b[i])

    @pl.loop(0, PART - 1)
    def _(i):
        summarise(part_near * PART + i + 1, mine * PART + i)
        near_b_copy(i + 1).start()
        own_step(i)

    summarise(mine * PART + PART - 1)
    own_step(PART - 1)

    def local(*heads):
        features = [silu(q[:, lanes(head)]) for head in heads]
        scores = [
            lax.dot_general(
                feature, k[:, lanes(head)], (((1,), (1,)), ((), ())),
                preferred_element_type=jnp.float32,
            )
            for feature, head in zip(features, heads)
        ]
        resumed = [
            jnp.dot(
                jnp.concatenate([feature * seg_masks[1], feature * seg_masks[2]], axis=1),
                jnp.concatenate([c[0, head], c[1, head]], axis=0),
                preferred_element_type=jnp.float32,
            )
            for feature, head in zip(features, heads)
        ]
        permitted = allowed[...]
        scores = [(score * permitted).astype(jnp.bfloat16) for score in scores]
        totals = [
            jnp.dot(score, v[:, lanes(head)], preferred_element_type=jnp.float32) + term
            for score, head, term in zip(scores, heads, resumed)
        ]
        first_only = [feature * seg_masks[0] for feature in features]
        for head, feature, total in zip(heads, first_only, totals):
            q[:, lanes(head)] = feature
            o[:, lanes(head)] = total

    def cross(*heads):
        totals = []
        for head in heads:
            wide = incoming[head]
            high = wide.astype(jnp.bfloat16)
            low = (wide - high.astype(jnp.float32)).astype(jnp.bfloat16)
            query = q[:, lanes(head)]
            totals.append(
                o[:, lanes(head)]
                + jnp.dot(
                    jnp.concatenate([query, query], axis=1),
                    jnp.concatenate([high, low], axis=0),
                    preferred_element_type=jnp.float32,
                )
            )
        squares = acc[...]
        for total in totals:
            squares = squares + total * total
        acc[...] = squares
        for head, total in zip(heads, totals):
            o[:, lanes(head)] = total

    def pair(chip_state, head, near):
        keep = coefs[1, 0:1, :]
        one = jnp.ones_like(keep)
        zero = jnp.zeros_like(keep)
        at_one = core == 1
        own = chip_state * jnp.where(at_one, keep, one) + near * jnp.where(at_one, one, zero)
        other = chip_state * jnp.where(at_one, one, keep) + state[head] * jnp.where(
            at_one, zero, one
        )
        return own, other

    def row_step(i):
        chip_copy(i).wait_recv()
        keep = coefs[4, 0:1, :]
        one = jnp.ones_like(keep)
        row[i] = chip_own[i] * jnp.where(y == 0, keep, one) + chip_in[i] * jnp.where(
            y == 0, one, keep
        )

    def prefix_step(i):
        @pl.when(z > 0)
        def _():
            z_copy(i).wait_recv()

        before = z_in[i]
        z_out[i] = row[i] + before * coefs[5, 0:1, :]

        @pl.when(z < depth - 1)
        def _():
            z_copy(i).start()

        keep = coefs[3, 0:1, :]
        one = jnp.ones_like(keep)
        zero = jnp.zeros_like(keep)
        at_one = y == 1
        back_out[i] = before * jnp.where(at_one, one, keep) + chip_own[i] * jnp.where(
            at_one, zero, one
        )
        back_copy(i).start()
        chip_state = before * jnp.where(at_one, keep, one) + chip_in[i] * jnp.where(
            at_one, one, zero
        )
        head = mine * PART + i
        own, other = pair(chip_state, head, near_b[i])
        final_a[i] = other
        final_a_send(i).start()
        incoming[head] = own

    def near_step(i):
        final_a_recv(i).wait_recv()
        cross(mine * PART + i, part_near * PART + i)

    def back_step(i):
        back_copy(i).wait_recv()
        head = part_far * PART + i
        own, other = pair(back_in[i], head, near_a[i])
        final_b[i] = other
        final_b_send(i).start()
        incoming[head] = own

    def diag_step(i):
        final_b_recv(i).wait_recv()
        cross(part_far * PART + i, part_diag * PART + i)

    skew = jnp.minimum(2 * z, 6)
    for i in range(4):
        q_loads[i].wait()

    @pl.loop(0, PART + LAG + 1)
    def _(t):
        @pl.when(t < PART)
        def _():
            local(mine * PART + t, part_near * PART + t)
            row_step(t)

        @pl.when((t >= PART) & (t < 2 * PART))
        def _():
            local(part_far * PART + t - PART, part_diag * PART + t - PART)

        @pl.when((t >= skew) & (t < skew + PART))
        def _():
            prefix_step(t - skew)

        @pl.when((t >= skew + 1) & (t < skew + 1 + PART))
        def _():
            near_step(t - skew - 1)

        @pl.when((t >= LAG) & (t < LAG + PART))
        def _():
            back_step(t - LAG)

        @pl.when(t >= LAG + 1)
        def _():
            diag_step(t - LAG - 1)

    def out_copy(i):
        span = pl.ds(pl.multiple_of(i * ROWS_OUT, ROWS_OUT), ROWS_OUT)
        return pltpu.make_async_copy(obuf.at[span], out_hbm.at[span], out_sem.at[i])

    @pl.loop(0, rows // ROWS_OUT)
    def _(i):
        span = pl.ds(pl.multiple_of(i * ROWS_OUT, ROWS_OUT), ROWS_OUT)
        square = jnp.sum(acc[span, :], axis=1, keepdims=True) * (1.0 / (HEADS * DIM))
        scale = lax.rsqrt(square + EPSILON)
        obuf[span, :] = (o[span, :] * scale * gain[...]).astype(jnp.bfloat16)
        out_copy(i).start()

    near_flag.wait_send()
    across_flag.wait_send()

    @pl.loop(0, PART)
    def _(i):
        near_a_copy(i).wait_send()
        near_b_copy(i).wait_send()
        chip_copy(i).wait_send()

        @pl.when(z < depth - 1)
        def _():
            z_copy(i).wait_send()

        back_copy(i).wait_send()
        final_a_send(i).wait_send()
        final_b_send(i).wait_send()

    @pl.loop(0, rows // ROWS_OUT)
    def _(i):
        out_copy(i).wait()


def on_device(queries, keys, values, doc_starts, previous_window_states, out_gain):
    rows, width = queries.shape
    bf16, f32 = jnp.bfloat16, jnp.float32
    part = pltpu.VMEM((PART, DIM, DIM), f32)
    everywhere = pl.BlockSpec(memory_space=pl.ANY)
    return pl.pallas_call(
        kernel,
        out_shape=jax.ShapeDtypeStruct((rows, width), bf16),
        in_specs=[pl.BlockSpec(memory_space=pltpu.SMEM)] + [everywhere] * 4
        + [pl.BlockSpec(memory_space=pltpu.VMEM)],
        out_specs=everywhere,
        scratch_shapes=[
            pltpu.VMEM((rows, width), bf16),
            pltpu.VMEM((rows, width), bf16),
            pltpu.VMEM((rows, width), bf16),
            pltpu.VMEM((2, HEADS, DIM, DIM), bf16),
            pltpu.VMEM((rows, width), f32),
            pltpu.VMEM((rows, width), bf16),
            pltpu.VMEM((rows, DIM), f32),
            pltpu.VMEM((rows, rows), f32),
            pltpu.VMEM((4, rows, DIM), bf16),
            pltpu.VMEM((4, 8, DIM), f32),
            pltpu.VMEM((6, 8, DIM), f32),
            pltpu.VMEM((HEADS, DIM, DIM), f32),
        ] + [part] * 12 + [
            pltpu.VMEM((HEADS, DIM, DIM), f32),
            pltpu.SemaphoreType.DMA((16,)),
            pltpu.SemaphoreType.DMA((rows // ROWS_OUT,)),
            pltpu.SemaphoreType.DMA((2,)),
            pltpu.SemaphoreType.DMA((2,)),
            pltpu.SemaphoreType.DMA((7, PART)),
            pltpu.SemaphoreType.DMA((7, PART)),
        ],
        compiler_params=pltpu.CompilerParams(
            collective_id=0, has_side_effects=True, vmem_limit_bytes=56 * 1024 * 1024
        ),
        cost_estimate=pl.CostEstimate(
            flops=4 * 10**9, bytes_accessed=13 * 10**6, transcendentals=3 * 10**6
        ),
    )(doc_starts, queries, keys, values, previous_window_states, out_gain.reshape(1, width))


def solution(mesh):
    placed = (
        P(("groups", "seq"), None),
        P(("groups", "seq"), None),
        P(("groups", "seq"), None),
        P(("groups", "seq"), None),
        P(("groups", "seq"), None, None, None),
        P(),
    )
    return jax.shard_map(
        on_device, mesh=mesh, in_specs=placed, out_specs=P(("groups", "seq"), None), check_vma=False
    )
```

```python
import jax
import jax.numpy as jnp
from jax import lax
from jax.experimental import pallas as pl
from jax.experimental.pallas import tpu as pltpu
from jax.sharding import PartitionSpec as P

HEADS = 32
DIM = 128
PART = HEADS // 4
EPSILON = 1e-06
LAG = 9
ROWS_OUT = 32
MESH = pl.DeviceIdType.MESH


def silu(x):
    half = x.astype(jnp.float32) * 0.5
    return (half + half * jnp.tanh(half)).astype(jnp.bfloat16)


def kernel(
    starts, q_hbm, k_hbm, v_hbm, c_hbm, gain, out_hbm,
    q, k, v, c, o, obuf, acc, allowed, seg_masks, flags, coefs,
    state, near_a, near_b, chip_out, chip_own, chip_in, row, z_in, z_out, back_out, back_in,
    final_a, final_b, incoming,
    in_sem, out_sem, flag_send, flag_recv, send_sem, recv_sem,
):
    rows = q.shape[0]
    count = lax.axis_size("seq")
    me = lax.axis_index("seq")
    z = me // 4
    depth = count // 4
    y = (me // 2) % 2
    core = me % 2
    partner = me + 1 - 2 * core
    across = me + 2 - 4 * y
    following = lax.rem(me + 4, count)
    mine = y * 2 + core
    part_near = y * 2 + (1 - core)
    part_far = (1 - y) * 2 + core
    part_diag = (1 - y) * 2 + (1 - core)

    def load(slot, source, target, part):
        columns = pl.ds(pl.multiple_of(part * (PART * DIM), PART * DIM), PART * DIM)
        return pltpu.make_async_copy(source.at[:, columns], target.at[:, columns], in_sem.at[slot])

    def load_states(slot, part):
        heads = pl.ds(part * PART, PART)
        return pltpu.make_async_copy(c_hbm.at[:, heads], c.at[:, heads], in_sem.at[slot])

    order_kv = (part_diag, part_far, part_near, mine)
    order_q = (mine, part_near, part_far, part_diag)
    k_loads = [load(i, k_hbm, k, p) for i, p in enumerate(order_kv)]
    v_loads = [load(4 + i, v_hbm, v, p) for i, p in enumerate(order_kv)]
    c_loads = [load_states(8 + i, p) for i, p in enumerate(order_kv)]
    q_loads = [load(12 + i, q_hbm, q, p) for i, p in enumerate(order_q)]
    for i in range(4):
        k_loads[i].start()
        v_loads[i].start()
        c_loads[i].start()
    for i in range(4):
        q_loads[i].start()

    barrier = pltpu.get_barrier_semaphore()
    for other in (partner, across):
        pl.semaphore_signal(barrier, inc=1, device_id={"seq": other}, device_id_type=MESH)

    @pl.when(z > 0)
    def _():
        pl.semaphore_signal(barrier, inc=1, device_id={"seq": me - 4}, device_id_type=MESH)

    @pl.when(z < depth - 1)
    def _():
        pl.semaphore_signal(barrier, inc=1, device_id={"seq": me + 4}, device_id_type=MESH)

    first, second = starts[0, 0], starts[0, 1]
    last = (first < rows).astype(jnp.int32) + (second < rows).astype(jnp.int32)
    take_one = jnp.where(last == 1, 1.0, 0.0)
    take_two = jnp.where(last == 2, 1.0, 0.0)
    here = jnp.where(last > 0, 1.0, 0.0)

    def segments(shape, dim):
        position = lax.broadcasted_iota(jnp.int32, shape, dim)
        one = jnp.where(position >= first, 1, 0)
        return position, one + jnp.where(position >= second, 1, 0)

    row_pos, row_seg = segments((rows, rows), 0)
    col_pos, col_seg = segments((rows, rows), 1)
    allowed[...] = jnp.where((row_pos >= col_pos) & (row_seg == col_seg), 1.0, 0.0)
    _, seg = segments((rows, DIM), 0)
    for i in range(3):
        seg_masks[i] = jnp.where(seg == i, 1.0, 0.0).astype(jnp.bfloat16)
    seg_masks[3] = jnp.where(seg == last, 1.0, 0.0).astype(jnp.bfloat16)
    acc[...] = jnp.zeros_like(acc)
    flags[0] = jnp.full((8, DIM), here, jnp.float32)

    @pl.when(z == 0)
    def _():
        z_in[...] = jnp.zeros_like(z_in)

    neighbours = 2 + jnp.where(z > 0, 1, 0) + jnp.where(z < depth - 1, 1, 0)
    pl.semaphore_wait(barrier, neighbours)

    def remote(kind, slot, source, target, device):
        return pltpu.make_async_remote_copy(
            src_ref=source, dst_ref=target, send_sem=send_sem.at[kind, slot],
            recv_sem=recv_sem.at[kind, slot], device_id={"seq": device}, device_id_type=MESH,
        )

    def flag_copy(slot, source, target, device):
        return pltpu.make_async_remote_copy(
            src_ref=flags.at[source], dst_ref=flags.at[target], send_sem=flag_send.at[slot],
            recv_sem=flag_recv.at[slot], device_id={"seq": device}, device_id_type=MESH,
        )

    def near_a_copy(i):
        return remote(0, i, state.at[part_diag * PART + i], near_a.at[i], partner)

    def near_b_copy(i):
        return remote(1, i, state.at[part_near * PART + i], near_b.at[i], partner)

    def chip_copy(i):
        return remote(2, i, chip_out.at[i], chip_in.at[i], across)

    def z_copy(i):
        return remote(3, i, z_out.at[i], z_in.at[i], following)

    def back_copy(i):
        return remote(4, i, back_out.at[i], back_in.at[i], across)

    def final_a_send(i):
        return remote(5, i, final_a.at[i], incoming.at[mine * PART + i], partner)

    def final_a_recv(i):
        return remote(5, i, final_a.at[i], incoming.at[part_near * PART + i], partner)

    def final_b_send(i):
        return remote(6, i, final_b.at[i], incoming.at[part_far * PART + i], partner)

    def final_b_recv(i):
        return remote(6, i, final_b.at[i], incoming.at[part_diag * PART + i], partner)

    near_flag = flag_copy(0, 0, 1, partner)
    near_flag.start()

    def lanes(head):
        return pl.ds(pl.multiple_of(head * DIM, DIM), DIM)

    def summarise(*heads):
        features = [silu(k[:, lanes(head)]) for head in heads]
        tails = [feature * seg_masks[3] for feature in features]
        totals = [
            lax.dot_general(
                tail, v[:, lanes(head)], (((0,), (0,)), ((), ())),
                preferred_element_type=jnp.float32,
            )
            + take_one * c[0, head].astype(jnp.float32)
            + take_two * c[1, head].astype(jnp.float32)
            for tail, head in zip(tails, heads)
        ]
        for head, feature, total in zip(heads, features, totals):
            k[:, lanes(head)] = feature
            state[head] = total

    def arrive(i):
        k_loads[i].wait()
        v_loads[i].wait()
        c_loads[i].wait()

    arrive(0)
    summarise(part_diag * PART)
    near_a_copy(0).start()
    arrive(1)

    near_flag.wait_recv()
    is_one = jnp.where(core == 1, 1.0, 0.0)
    keep_me = 1.0 - flags[0]
    keep_near = 1.0 - flags[1]
    coefs[0] = jnp.where(core == 1, keep_me, keep_near)
    coefs[1] = jnp.where(core == 1, keep_near, keep_me)
    coefs[2] = keep_me * keep_near
    flags[2] = keep_me * keep_near
    across_flag = flag_copy(1, 2, 3, across)
    across_flag.start()

    def chip_sum(head, near):
        keep = coefs[0, 0:1, :]
        own_scale = jnp.where(core == 1, jnp.ones_like(keep), keep)
        near_scale = jnp.where(core == 1, keep, jnp.ones_like(keep))
        return state[head] * own_scale + near * near_scale

    def chip_step(i):
        near_a_copy(i).wait_recv()
        chip_out[i] = chip_sum(part_far * PART + i, near_a[i])
        chip_copy(i).start()

    @pl.loop(0, PART - 1)
    def _(i):
        summarise(part_diag * PART + i + 1, part_far * PART + i)
        near_a_copy(i + 1).start()
        chip_step(i)

    summarise(part_far * PART + PART - 1)
    chip_step(PART - 1)

    arrive(2)
    arrive(3)
    summarise(part_near * PART)
    near_b_copy(0).start()
    across_flag.wait_recv()
    own_keep = coefs[2]
    far_keep = flags[3]
    coefs[3] = jnp.where(y == 0, own_keep, far_keep)
    coefs[4] = jnp.where(y == 0, far_keep, own_keep)
    coefs[5] = own_keep * far_keep

    def own_step(i):
        near_b_copy(i).wait_recv()
        chip_own[i] = chip_sum(mine * PART + i, near_b[i])

    @pl.loop(0, PART - 1)
    def _(i):
        summarise(part_near * PART + i + 1, mine * PART + i)
        near_b_copy(i + 1).start()
        own_step(i)

    summarise(mine * PART + PART - 1)
    own_step(PART - 1)

    def local(*heads):
        features = [silu(q[:, lanes(head)]) for head in heads]
        scores = [
            lax.dot_general(
                feature, k[:, lanes(head)], (((1,), (1,)), ((), ())),
                preferred_element_type=jnp.float32,
            )
            for feature, head in zip(features, heads)
        ]
        resumed = [
            jnp.dot(
                jnp.concatenate([feature * seg_masks[1], feature * seg_masks[2]], axis=1),
                jnp.concatenate([c[0, head], c[1, head]], axis=0),
                preferred_element_type=jnp.float32,
            )
            for feature, head in zip(features, heads)
        ]
        permitted = allowed[...]
        scores = [(score * permitted).astype(jnp.bfloat16) for score in scores]
        totals = [
            jnp.dot(score, v[:, lanes(head)], preferred_element_type=jnp.float32) + term
            for score, head, term in zip(scores, heads, resumed)
        ]
        first_only = [feature * seg_masks[0] for feature in features]
        for head, feature, total in zip(heads, first_only, totals):
            q[:, lanes(head)] = feature
            o[:, lanes(head)] = total

    def cross(*heads):
        totals = []
        for head in heads:
            wide = incoming[head]
            high = wide.astype(jnp.bfloat16)
            low = (wide - high.astype(jnp.float32)).astype(jnp.bfloat16)
            query = q[:, lanes(head)]
            totals.append(
                o[:, lanes(head)]
                + jnp.dot(
                    jnp.concatenate([query, query], axis=1),
                    jnp.concatenate([high, low], axis=0),
                    preferred_element_type=jnp.float32,
                )
            )
        squares = acc[...]
        for total in totals:
            squares = squares + total * total
        acc[...] = squares
        for head, total in zip(heads, totals):
            o[:, lanes(head)] = total

    def pair(chip_state, head, near):
        keep = coefs[1, 0:1, :]
        one = jnp.ones_like(keep)
        zero = jnp.zeros_like(keep)
        at_one = core == 1
        own = chip_state * jnp.where(at_one, keep, one) + near * jnp.where(at_one, one, zero)
        other = chip_state * jnp.where(at_one, one, keep) + state[head] * jnp.where(
            at_one, zero, one
        )
        return own, other

    def row_step(i):
        chip_copy(i).wait_recv()
        keep = coefs[4, 0:1, :]
        one = jnp.ones_like(keep)
        row[i] = chip_own[i] * jnp.where(y == 0, keep, one) + chip_in[i] * jnp.where(
            y == 0, one, keep
        )

    def prefix_step(i):
        @pl.when(z > 0)
        def _():
            z_copy(i).wait_recv()

        before = z_in[i]
        z_out[i] = row[i] + before * coefs[5, 0:1, :]

        @pl.when(z < depth - 1)
        def _():
            z_copy(i).start()

        keep = coefs[3, 0:1, :]
        one = jnp.ones_like(keep)
        zero = jnp.zeros_like(keep)
        at_one = y == 1
        back_out[i] = before * jnp.where(at_one, one, keep) + chip_own[i] * jnp.where(
            at_one, zero, one
        )
        back_copy(i).start()
        chip_state = before * jnp.where(at_one, keep, one) + chip_in[i] * jnp.where(
            at_one, one, zero
        )
        head = mine * PART + i
        own, other = pair(chip_state, head, near_b[i])
        final_a[i] = other
        final_a_send(i).start()
        incoming[head] = own

    def near_step(i):
        final_a_recv(i).wait_recv()
        cross(mine * PART + i, part_near * PART + i)

    def back_step(i):
        back_copy(i).wait_recv()
        head = part_far * PART + i
        own, other = pair(back_in[i], head, near_a[i])
        final_b[i] = other
        final_b_send(i).start()
        incoming[head] = own

    def diag_step(i):
        final_b_recv(i).wait_recv()
        cross(part_far * PART + i, part_diag * PART + i)

    skew = jnp.minimum(2 * z, 6)
    for i in range(4):
        q_loads[i].wait()

    @pl.loop(0, PART + LAG + 1)
    def _(t):
        @pl.when(t < PART)
        def _():
            row_step(t)

        @pl.when((t >= skew) & (t < skew + PART))
        def _():
            prefix_step(t - skew)

        @pl.when((t >= LAG) & (t < LAG + PART))
        def _():
            back_step(t - LAG)

        @pl.when(t < PART)
        def _():
            local(mine * PART + t, part_near * PART + t)

        @pl.when((t >= PART) & (t < 2 * PART))
        def _():
            local(part_far * PART + t - PART, part_diag * PART + t - PART)

        @pl.when((t >= skew + 1) & (t < skew + 1 + PART))
        def _():
            near_step(t - skew - 1)

        @pl.when(t >= LAG + 1)
        def _():
            diag_step(t - LAG - 1)

    def out_copy(i):
        span = pl.ds(pl.multiple_of(i * ROWS_OUT, ROWS_OUT), ROWS_OUT)
        return pltpu.make_async_copy(obuf.at[span], out_hbm.at[span], out_sem.at[i])

    @pl.loop(0, rows // ROWS_OUT)
    def _(i):
        span = pl.ds(pl.multiple_of(i * ROWS_OUT, ROWS_OUT), ROWS_OUT)
        square = jnp.sum(acc[span, :], axis=1, keepdims=True) * (1.0 / (HEADS * DIM))
        scale = lax.rsqrt(square + EPSILON)
        obuf[span, :] = (o[span, :] * scale * gain[...]).astype(jnp.bfloat16)
        out_copy(i).start()

    near_flag.wait_send()
    across_flag.wait_send()

    @pl.loop(0, PART)
    def _(i):
        near_a_copy(i).wait_send()
        near_b_copy(i).wait_send()
        chip_copy(i).wait_send()

        @pl.when(z < depth - 1)
        def _():
            z_copy(i).wait_send()

        back_copy(i).wait_send()
        final_a_send(i).wait_send()
        final_b_send(i).wait_send()

    @pl.loop(0, rows // ROWS_OUT)
    def _(i):
        out_copy(i).wait()


def on_device(queries, keys, values, doc_starts, previous_window_states, out_gain):
    rows, width = queries.shape
    bf16, f32 = jnp.bfloat16, jnp.float32
    part = pltpu.VMEM((PART, DIM, DIM), f32)
    everywhere = pl.BlockSpec(memory_space=pl.ANY)
    return pl.pallas_call(
        kernel,
        out_shape=jax.ShapeDtypeStruct((rows, width), bf16),
        in_specs=[pl.BlockSpec(memory_space=pltpu.SMEM)] + [everywhere] * 4
        + [pl.BlockSpec(memory_space=pltpu.VMEM)],
        out_specs=everywhere,
        scratch_shapes=[
            pltpu.VMEM((rows, width), bf16),
            pltpu.VMEM((rows, width), bf16),
            pltpu.VMEM((rows, width), bf16),
            pltpu.VMEM((2, HEADS, DIM, DIM), bf16),
            pltpu.VMEM((rows, width), f32),
            pltpu.VMEM((rows, width), bf16),
            pltpu.VMEM((rows, DIM), f32),
            pltpu.VMEM((rows, rows), f32),
            pltpu.VMEM((4, rows, DIM), bf16),
            pltpu.VMEM((4, 8, DIM), f32),
            pltpu.VMEM((6, 8, DIM), f32),
            pltpu.VMEM((HEADS, DIM, DIM), f32),
        ] + [part] * 12 + [
            pltpu.VMEM((HEADS, DIM, DIM), f32),
            pltpu.SemaphoreType.DMA((16,)),
            pltpu.SemaphoreType.DMA((rows // ROWS_OUT,)),
            pltpu.SemaphoreType.DMA((2,)),
            pltpu.SemaphoreType.DMA((2,)),
            pltpu.SemaphoreType.DMA((7, PART)),
            pltpu.SemaphoreType.DMA((7, PART)),
        ],
        compiler_params=pltpu.CompilerParams(
            collective_id=0, has_side_effects=True, vmem_limit_bytes=56 * 1024 * 1024
        ),
        cost_estimate=pl.CostEstimate(
            flops=4 * 10**9, bytes_accessed=13 * 10**6, transcendentals=3 * 10**6
        ),
    )(doc_starts, queries, keys, values, previous_window_states, out_gain.reshape(1, width))


def solution(mesh):
    placed = (
        P(("groups", "seq"), None),
        P(("groups", "seq"), None),
        P(("groups", "seq"), None),
        P(("groups", "seq"), None),
        P(("groups", "seq"), None, None, None),
        P(),
    )
    return jax.shard_map(
        on_device, mesh=mesh, in_specs=placed, out_specs=P(("groups", "seq"), None), check_vma=False
    )
```
